512 devices in a mesh: row: 64 (over y_lo, z, core), col: 8 (over x, y_hi).
Axes of the slice: x: 4, y: 4 (y_hi: 2, y_lo: 2; y = y_hi * 2 + y_lo), z: 16, core: 2. Of those that a mesh axis runs over, the one named last changes fastest.
Arguments:
- mantissas: bfloat16 [512, 6144], P('row', 'col'), may hold values from -4 to 4
- block_exponents: int32 [512, 48], P('row', 'col'), may hold values from -2 to 1
- input_weight: bfloat16 [6144, 24576], P('col', 'row'), may hold values from -0.078125 to 0.078125
- input_noise: bfloat16 [6144, 24576], P('col', 'row'), may hold values from -0.0546875 to 0.0546875
- output_weight: bfloat16 [24576, 6144], P('row', 'col'), may hold values from -0.0390625 to 0.0390625
- output_noise: bfloat16 [24576, 6144], P('row', 'col'), may hold values from -0.02734375 to 0.02734375
- preactivation: bfloat16 [512, 24576], P(None, 'row'), may hold values from -6 to 6
- adc_mask: int32 [512, 192], P(None, 'row'), may hold values 0 or 1
- teacher: bfloat16 [512, 6144], P('row', 'col'), may hold values from -6 to 6
Outputs:
- input_grad: bfloat16 [512, 6144], P('row', 'col')
- first_grad: bfloat16 [6144, 24576], P('col', 'row')
- second_grad: bfloat16 [24576, 6144], P('row', 'col')
The draws below stay inside these ranges and needn't reach their ends.
All inputs are finite; a program needn't handle non-finite values. No bound on the sum of `adc_mask` on one device may be relied on, other than what follows from the above.
Results may differ from the reference program's by a relative error of at most 0.022.
Values may be sent and summed in bfloat16 or wider, within the bound.
No kernel may reach another device: no remote copies, remote signals or barrier semaphores. Data moves between devices by JAX's collectives and lax.ppermute only.
A program may use at most 64 MiB of HBM per device.

```python
import jax
import jax.numpy as jnp

D = 6144
FF = 24576
BLOCK = 128
TILE = 128
TOKENS = 512


def set_ends(drawn, own_key, low, top_value):
    dims = drawn.shape
    spot = [jax.random.randint(jax.random.fold_in(own_key, axis), (), 0, dims[axis]) for axis in range(len(dims))]
    drawn = drawn.at[tuple(spot)].set(low)
    longest = dims.index(max(dims))
    spot[longest] = (spot[longest] + 1) % dims[longest]
    return drawn.at[tuple(spot)].set(top_value)


def steps_of(key, extent, pieces, least, largest):
    def one(dim, parts):
        draws = jax.random.uniform(jax.random.fold_in(jax.random.fold_in(key, 6), dim), (parts,), jnp.float32, least / len(pieces), largest / len(pieces))
        return jnp.repeat(jnp.exp(draws), extent[dim] // parts).reshape((-1,) + (1,) * (len(extent) - dim - 1))

    factor_of = one(*pieces[0])
    for cut in pieces[1:]:
        factor_of = factor_of * one(*cut)
    return factor_of


def noise(key, dims, spread, limit, split=(), held_as=jnp.bfloat16):
    factor_of = steps_of(key, dims, split, -0.22, 0.18) if split else 1.0
    array = jax.random.normal(key, dims, jnp.float32) * spread * factor_of
    return jnp.minimum(jnp.maximum(array, -limit), limit).astype(held_as)


def setup_inputs(seed: int = 0) -> dict:
    splits = jax.random.split(jax.random.key(seed), 10)
    mantissas = noise(splits[0], (TOKENS, D), 1.0, 4.0, ((0, 64), (1, 8)))
    block_exponents = set_ends(jax.random.randint(splits[1], (TOKENS, D // BLOCK), -2, 2), jax.random.fold_in(splits[1], 1), -2, 1).astype(jnp.int32)
    input_weight = noise(splits[2], (D, FF), D ** -0.5, 0.078125, ((0, 8), (1, 64)))
    input_noise = noise(splits[3], (D, FF), (0.3 * D ** -0.5), 0.0546875, ((0, 8), (1, 64)))
    output_weight = noise(splits[4], (FF, D), FF ** -0.5, 0.0390625, ((0, 64), (1, 8)))
    output_noise = noise(splits[5], (FF, D), (0.3 * FF ** -0.5), 0.02734375, ((0, 64), (1, 8)))
    preactivation = noise(splits[6], (TOKENS, FF), 1.0, 6.0, ((1, 64),))
    adc_mask = set_ends((jax.random.randint(splits[7], (TOKENS, FF // TILE), 0, 2) < 1).astype(jnp.int32), jax.random.fold_in(splits[7], 1), 0, 1)
    teacher = noise(splits[8], (TOKENS, D), 1.0, 6.0, ((0, 64), (1, 8)))
    return {"mantissas": mantissas, "block_exponents": block_exponents, "input_weight": input_weight, "input_noise": input_noise, "output_weight": output_weight, "output_noise": output_noise, "preactivation": preactivation, "adc_mask": adc_mask, "teacher": teacher}


adc_range = 1.5

def activation(hidden, mask):
    gelu = jax.nn.gelu(hidden, approximate=True)
    tiles = jnp.repeat(mask, TILE, axis=1)
    return jnp.where(tiles > 0, adc_range * jnp.tanh(gelu / adc_range), gelu)

def reference(mantissas, block_exponents, input_weight, input_noise, output_weight, output_noise, preactivation, adc_mask, teacher):
    scales = jnp.repeat(jnp.exp2(block_exponents.astype(jnp.float32)), BLOCK, axis=1)
    features = (mantissas.astype(jnp.float32) * scales).astype(jnp.bfloat16)
    noisy_in = (input_weight.astype(jnp.float32) + input_noise.astype(jnp.float32)).astype(jnp.bfloat16)
    noisy_out = (output_weight.astype(jnp.float32) + output_noise.astype(jnp.float32)).astype(jnp.bfloat16)
    hidden = preactivation.astype(jnp.float32)
    values, pullback = jax.vjp(lambda v: activation(v, adc_mask), hidden)
    activated = values.astype(jnp.bfloat16)
    student = jnp.dot(activated, noisy_out, preferred_element_type=jnp.float32)
    residual = (student - teacher.astype(jnp.float32)).astype(jnp.bfloat16)
    inverse_root = TOKENS ** (-0.5)
    second_grad = (jnp.dot(activated.T, residual, preferred_element_type=jnp.float32) * inverse_root).astype(jnp.bfloat16)
    hidden_back = jnp.dot(residual, noisy_out.T, preferred_element_type=jnp.float32)
    hidden_grad = pullback(hidden_back)[0].astype(jnp.bfloat16)
    first_grad = (jnp.dot(features.T, hidden_grad, preferred_element_type=jnp.float32) * inverse_root).astype(jnp.bfloat16)
    input_grad = jnp.dot(hidden_grad, noisy_in.T, preferred_element_type=jnp.float32).astype(jnp.bfloat16)
    return (input_grad, first_grad, second_grad)
```

```python
import jax
import jax.numpy as jnp
from jax import lax
from jax.sharding import PartitionSpec as P

adc_range = 1.5
bf16 = jnp.bfloat16
f32 = jnp.float32


def activation(hidden, mask):
    width = hidden.shape[1] // mask.shape[1]
    gelu = jax.nn.gelu(hidden, approximate=True)
    tiles = jnp.repeat(mask, width, axis=1)
    return jnp.where(tiles > 0, adc_range * jnp.tanh(gelu / adc_range), gelu)


def dot(a, b):
    return jnp.dot(a, b, preferred_element_type=f32)


def dot_t(a, b):
    return lax.dot_general(a, b, (((1,), (1,)), ((), ())), preferred_element_type=f32)


def t_dot(a, b):
    return lax.dot_general(a, b, (((0,), (0,)), ((), ())), preferred_element_type=f32)


def program(rows, cols):
    chips = rows // 2
    same_core = [[chip * 2 + core for chip in range(chips)] for core in range(2)]
    same_chip = [[chip * 2, chip * 2 + 1] for chip in range(chips)]
    swap = [(i, i ^ 1) for i in range(rows)]

    def by_core(a):
        total = a.shape[0]
        return a.reshape(chips, 2, total // rows, -1).swapaxes(0, 1).reshape(total, -1)

    def scatter_sum(left, right):
        core = lax.axis_index("row") % 2
        half = left.shape[0] // 2
        halves = left.reshape(2, half, -1)
        theirs = dot(lax.dynamic_index_in_dim(halves, 1 - core, 0, False), right)
        got = lax.ppermute(theirs.astype(bf16), "row", swap)
        ours = dot(lax.dynamic_index_in_dim(halves, core, 0, False), right)
        both = (ours + got.astype(f32)).astype(bf16).reshape(chips, half // chips, -1)
        parts = lax.all_to_all(both, "row", 0, 0, axis_index_groups=same_core, tiled=True)
        return jnp.sum(parts.astype(f32), axis=0)

    def local(
        mantissas,
        block_exponents,
        input_weight,
        input_noise,
        output_weight,
        output_noise,
        preactivation,
        adc_mask,
        teacher,
    ):
        block_width = mantissas.shape[1] // block_exponents.shape[1]
        scales = jnp.repeat(jnp.exp2(block_exponents.astype(f32)), block_width, axis=1)
        halved = lax.all_gather(mantissas.astype(f32) * (scales * 0.5), "row", axis=0, tiled=True)
        features = by_core((halved * 2.0).astype(bf16))
        noisy_in = (input_weight.astype(f32) + input_noise.astype(f32)).astype(bf16)
        noisy_out = (output_weight.astype(f32) + output_noise.astype(f32)).astype(bf16)
        hidden = by_core(preactivation)
        mask = by_core(adc_mask)
        tokens = hidden.shape[0]
        inverse_root = tokens ** (-0.5)
        activated = activation(hidden.astype(f32), mask).astype(bf16)

        student = scatter_sum(activated, noisy_out)
        residual = (student - teacher.astype(f32)).astype(bf16)
        piece = lax.all_to_all(
            jnp.broadcast_to(residual, (chips,) + residual.shape),
            "row",
            0,
            0,
            axis_index_groups=same_core,
            tiled=True,
        ).reshape(tokens // 2, -1)
        piece = lax.all_gather(piece, "row", axis=0, tiled=True, axis_index_groups=same_chip)

        fresh = dot_t(piece, noisy_out).astype(bf16).reshape(cols, tokens // cols, -1)
        second_grad = (t_dot(activated, piece) * inverse_root).astype(bf16)
        parts = lax.all_to_all(fresh, "col", 0, 0, tiled=True)
        summed = jnp.sum(parts.astype(f32), axis=0)
        share = tokens // cols
        start = lax.axis_index("col") * share
        own = lax.dynamic_slice_in_dim(hidden, start, share, 0).astype(f32)
        own_mask = lax.dynamic_slice_in_dim(mask, start, share, 0)
        pullback = jax.vjp(lambda v: activation(v, own_mask), own)[1]
        own_grad = pullback(summed)[0].astype(bf16)
        hidden_grad = lax.all_to_all(
            jnp.broadcast_to(own_grad, (cols,) + own_grad.shape), "col", 0, 0, tiled=True
        ).reshape(tokens, -1)
        input_grad = scatter_sum(hidden_grad, noisy_in.T).astype(bf16)
        first_grad = (t_dot(features, hidden_grad) * inverse_root).astype(bf16)
        return (input_grad, first_grad, second_grad)

    return local


def solution(mesh):
    placed = (
        P("row", "col"),
        P("row", "col"),
        P("col", "row"),
        P("col", "row"),
        P("row", "col"),
        P("row", "col"),
        P(None, "row"),
        P(None, "row"),
        P("row", "col"),
    )
    return jax.shard_map(
        program(mesh.shape["row"], mesh.shape["col"]),
        mesh=mesh,
        in_specs=placed,
        out_specs=(P("row", "col"), P("col", "row"), P("row", "col")),
        check_vma=False,
    )
```

```python
import jax
import jax.numpy as jnp
from jax import lax
from jax.sharding import PartitionSpec as P

adc_range = 1.5
bf16 = jnp.bfloat16
f32 = jnp.float32


def activation(hidden, mask):
    width = hidden.shape[1] // mask.shape[1]
    gelu = jax.nn.gelu(hidden, approximate=True)
    tiles = jnp.repeat(mask, width, axis=1)
    return jnp.where(tiles > 0, adc_range * jnp.tanh(gelu / adc_range), gelu)


def dot(a, b):
    return jnp.dot(a, b, preferred_element_type=f32)


def dot_t(a, b):
    return lax.dot_general(a, b, (((1,), (1,)), ((), ())), preferred_element_type=f32)


def t_dot(a, b):
    return lax.dot_general(a, b, (((0,), (0,)), ((), ())), preferred_element_type=f32)


def pick(a, i):
    return lax.dynamic_index_in_dim(a, i, 0, False)


def program(rows, cols):
    zs = rows // 4
    same_core = [[chip * 2 + core for chip in range(2 * zs)] for core in range(2)]
    along_z = [[(y * zs + z) * 2 + core for z in range(zs)] for y in range(2) for core in range(2)]
    swap_core = [(i, i ^ 1) for i in range(rows)]
    swap_y = [(i, (i + rows // 2) % rows) for i in range(rows)]

    def from_core(a):
        return lax.ppermute(a, "row", swap_core)

    def from_y(a):
        return lax.ppermute(a, "row", swap_y)

    def exchange(a, axis, groups=None):
        return lax.all_to_all(a, axis, 0, 0, axis_index_groups=groups, tiled=True)

    def spread(own, count, axis, groups=None):
        return exchange(jnp.broadcast_to(own, (count,) + own.shape), axis, groups)

    def add_up(parts):
        return jnp.sum(parts.astype(f32), axis=0)

    def of_four(own):
        pair = jnp.stack([own, from_y(own)])
        return jnp.concatenate([pair, from_core(pair)])

    def local(
        mantissas,
        block_exponents,
        input_weight,
        input_noise,
        output_weight,
        output_noise,
        preactivation,
        adc_mask,
        teacher,
    ):
        me = lax.axis_index("row")
        core, y = me % 2, me // (rows // 2)
        tokens, width = preactivation.shape
        model = mantissas.shape[1]
        quota = tokens // rows
        group = tokens // 4
        share = group // cols
        inverse_root = tokens ** (-0.5)

        block_width = model // block_exponents.shape[1]
        scales = jnp.repeat(jnp.exp2(block_exponents.astype(f32)), block_width, axis=1)
        features = (mantissas.astype(f32) * scales).astype(bf16)
        noisy_out = (output_weight.astype(f32) + output_noise.astype(f32)).astype(bf16)
        noisy_in = (input_weight.astype(f32) + input_noise.astype(f32)).astype(bf16)

        def by_group(a):
            return a.reshape(2, zs, 2, quota, -1).transpose(2, 0, 1, 3, 4)

        hidden = by_group(preactivation)
        mask = by_group(adc_mask)
        activated = activation(
            hidden.reshape(tokens, width).astype(f32), mask.reshape(tokens, -1)
        ).astype(bf16)

        pair = activated.reshape(2, 2 * group, width)
        theirs = from_core(dot(pick(pair, 1 - core), noisy_out).astype(bf16))
        both = dot(pick(pair, core), noisy_out) + theirs.astype(f32)
        both = both.astype(bf16).reshape(2 * zs, quota, model)
        student = add_up(exchange(both, "row", same_core))
        residual = (student - teacher.astype(f32)).astype(bf16)

        all_out = of_four(noisy_out).reshape(4 * width, model)
        all_in = of_four(noisy_in)
        all_in = jnp.concatenate([all_in[i] for i in range(4)], axis=1)
        first = lax.axis_index("col") * share
        own = lax.dynamic_slice_in_dim(hidden.reshape(4, group, width), first, share, 1)
        own_mask = lax.dynamic_slice_in_dim(mask.reshape(4, group, -1), first, share, 1)
        own_mask = own_mask.reshape(4 * share, -1)
        own = own.reshape(4 * share, width).astype(f32)
        slope = jax.vjp(lambda v: activation(v, own_mask), own)[1](jnp.ones_like(own))[0]
        slope = slope.reshape(2, 2, share, width).swapaxes(0, 1)
        slope = jnp.stack([pick(slope, y), from_y(pick(slope, 1 - y))], axis=1)
        slope = jnp.concatenate([pick(slope, core), from_core(pick(slope, 1 - core))])
        slope = slope.swapaxes(0, 1).reshape(share, 4 * width)

        sent = jnp.concatenate([residual, features])
        got = spread(sent, zs, "row", along_z)
        piece = got[:, :quota].reshape(group, model)
        fresh = dot_t(piece, all_out).astype(bf16).reshape(cols, share, 4 * width)
        own_grad = (add_up(exchange(fresh, "col")) * slope).astype(bf16)
        hidden_grad = spread(own_grad, cols, "col").reshape(group, 4 * width)

        partial = dot_t(hidden_grad, all_in).astype(bf16).reshape(zs, quota, model)
        input_grad = add_up(exchange(partial, "row", along_z)).astype(bf16)

        all_got = of_four(got)
        all_piece = all_got[:, :, :quota].reshape(tokens, model)
        all_features = all_got[:, :, quota:].reshape(tokens, model)
        near = pick(activated.reshape(2, 2, group, width), core)
        far = pick(activated.reshape(2, 2, group, width), 1 - core)
        all_activated = jnp.concatenate(
            [pick(near, y), pick(near, 1 - y), pick(far, y), pick(far, 1 - y)]
        )
        second_grad = (t_dot(all_activated, all_piece) * inverse_root).astype(bf16)

        blocks = [hidden_grad[:, i * width : (i + 1) * width] for i in range(4)]
        over = from_y(jnp.stack([blocks[1], blocks[3]]))
        other = from_core(jnp.stack([blocks[2], over[1]]))
        all_grad = jnp.concatenate([blocks[0], over[0], other[0], other[1]])
        first_grad = (t_dot(all_features, all_grad) * inverse_root).astype(bf16)
        return (input_grad, first_grad, second_grad)

    return local


def solution(mesh):
    placed = (
        P("row", "col"),
        P("row", "col"),
        P("col", "row"),
        P("col", "row"),
        P("row", "col"),
        P("row", "col"),
        P(None, "row"),
        P(None, "row"),
        P("row", "col"),
    )
    return jax.shard_map(
        program(mesh.shape["row"], mesh.shape["col"]),
        mesh=mesh,
        in_specs=placed,
        out_specs=(P("row", "col"), P("col", "row"), P("row", "col")),
        check_vma=False,
    )
```

```python
import functools

import jax
import jax.numpy as jnp
from jax import lax
from jax.experimental import pallas as pl
from jax.experimental.pallas import tpu as pltpu
from jax.sharding import PartitionSpec as P

adc_range = 1.5
bf16 = jnp.bfloat16
f32 = jnp.float32


def activation(hidden, mask):
    width = hidden.shape[1] // mask.shape[1]
    gelu = jax.nn.gelu(hidden, approximate=True)
    tiles = jnp.repeat(mask, width, axis=1)
    return jnp.where(tiles > 0, adc_range * jnp.tanh(gelu / adc_range), gelu)


def dot(a, b):
    return jnp.dot(a, b, preferred_element_type=f32)


def dot_t(a, b):
    return lax.dot_general(a, b, (((1,), (1,)), ((), ())), preferred_element_type=f32)


def t_dot(a, b):
    return lax.dot_general(a, b, (((0,), (0,)), ((), ())), preferred_element_type=f32)


def pick(a, i):
    return lax.dynamic_index_in_dim(a, i, 0, False)


whole = pl.BlockSpec(memory_space=pltpu.VMEM)
scalar = pl.BlockSpec(memory_space=pltpu.SMEM)
anywhere = pl.BlockSpec(memory_space=pl.ANY)
params = pltpu.CompilerParams(vmem_limit_bytes=40 * 2**20)


def shape(*dims):
    return jax.ShapeDtypeStruct(dims, bf16)


def start_kernel(quota, core_ref, pre_ref, mask_ref, w_ref, n_ref, act_ref, out_ref, theirs_ref):
    out_ref[...] = (w_ref[...].astype(f32) + n_ref[...].astype(f32)).astype(bf16)
    tokens, width = pre_ref.shape
    tiles = mask_ref.shape[1]
    tile = width // tiles
    step = min(128, tokens)
    for first in range(0, tokens, step):
        for j in range(tiles):
            columns = slice(j * tile, (j + 1) * tile)
            hidden = pre_ref[first : first + step, columns].astype(f32)
            gelu = jax.nn.gelu(hidden, approximate=True)
            value = jnp.where(
                mask_ref[first : first + step, j : j + 1] > 0,
                adc_range * jnp.tanh(gelu / adc_range),
                gelu,
            )
            value = value.reshape(step // (2 * quota), 2, quota, tile)
            for c in range(2):
                part = value[:, c].reshape(step // 2, tile).astype(bf16)
                act_ref[c, first // 2 : (first + step) // 2, columns] = part
    theirs = dot(act_ref[1 - core_ref[0]], out_ref[...])
    theirs_ref[...] = theirs.astype(bf16)


def residual_kernel(parts_ref, teacher_ref, features_ref, *refs):
    out_ref = refs[-1]
    total = parts_ref[0].astype(f32)
    for i in range(1, parts_ref.shape[0]):
        total += parts_ref[i].astype(f32)
    residual = (total - teacher_ref[...].astype(f32)).astype(bf16)
    block = jnp.concatenate([residual.astype(f32), features_ref[...].astype(f32)]).astype(bf16)
    for i in range(out_ref.shape[0]):
        out_ref[i] = block


def rows_kernel(got_ref, rows_ref):
    count, twice, model = got_ref.shape
    got = got_ref[...].astype(f32)
    for i in range(2):
        half = got[:, i * twice // 2 : (i + 1) * twice // 2].reshape(count * twice // 2, model)
        rows_ref[:, i * model : (i + 1) * model] = half.astype(bf16)


def input_kernel(grad_ref, a_ref, b_ref, c_ref, d_ref, partial_ref, *refs):
    width = a_ref.shape[1]
    block = [grad_ref[:, i * width : (i + 1) * width] for i in range(4)]
    total = dot_t(block[0], a_ref[...])
    for one, ref in zip(block[1:], (b_ref, c_ref, d_ref)):
        total += dot_t(one, ref[...])
    partial_ref[...] = total.astype(bf16)
    for one, ref in zip(block[1:], refs):
        ref[...] = one


def pair_kernel(a_ref, b_ref, after_ref, pair_ref):
    pair_ref[0] = a_ref[...]
    pair_ref[1] = b_ref[...]


def grads_kernel(scale, at_ref, act_ref, grad_ref, near_ref, far_ref, y_ref, core_ref, both_ref, first_ref, second_ref):
    width, model = second_ref.shape
    c, y = at_ref[0], at_ref[1]
    act = [act_ref[c, y], act_ref[c, 1 - y], act_ref[1 - c, y], act_ref[1 - c, 1 - y]]
    rows = [(ref, i) for ref in (near_ref, far_ref) for i in range(2)]
    residual = [ref[i, :, :model] for ref, i in rows]
    features = [ref[i, :, model:] for ref, i in rows]
    grad = [grad_ref[:, :width]] + [ref[...] for ref in (y_ref, core_ref, both_ref)]
    second = t_dot(jnp.concatenate(act), jnp.concatenate(residual))
    second_ref[...] = (second * scale).astype(bf16)
    first = t_dot(jnp.concatenate(features), jnp.concatenate(grad))
    first_ref[...] = (first * scale).astype(bf16)


def program(rows, cols):
    zs = rows // 4
    same_core = [[chip * 2 + core for chip in range(2 * zs)] for core in range(2)]
    along_z = [[(y * zs + z) * 2 + core for z in range(zs)] for y in range(2) for core in range(2)]
    swap_core = [(i, i ^ 1) for i in range(rows)]
    swap_both = [(i, (i ^ 1) + (rows // 2 if i < rows // 2 else -(rows // 2))) for i in range(rows)]
    swap_y = [(i, (i + rows // 2) % rows) for i in range(rows)]

    def from_core(a):
        return lax.ppermute(a, "row", swap_core)

    def from_y(a):
        return lax.ppermute(a, "row", swap_y)

    def from_both(a):
        return lax.ppermute(a, "row", swap_both)

    def exchange(a, axis, groups=None):
        return lax.all_to_all(a, axis, 0, 0, axis_index_groups=groups, tiled=True)

    def spread(own, count, axis, groups=None):
        return exchange(jnp.broadcast_to(own, (count,) + own.shape), axis, groups)

    def add_up(parts):
        return jnp.sum(parts.astype(f32), axis=0)

    def of_four(own):
        pair = jnp.stack([own, from_y(own)])
        return jnp.concatenate([pair, from_core(pair)])

    def local(
        mantissas,
        block_exponents,
        input_weight,
        input_noise,
        output_weight,
        output_noise,
        preactivation,
        adc_mask,
        teacher,
    ):
        me = lax.axis_index("row")
        core, y = me % 2, me // (rows // 2)
        tokens, width = preactivation.shape
        model = mantissas.shape[1]
        quota = tokens // rows
        group = tokens // 4
        share = group // cols
        inverse_root = tokens ** (-0.5)

        block_width = model // block_exponents.shape[1]
        scales = jnp.repeat(jnp.exp2(block_exponents.astype(f32)), block_width, axis=1)
        features = (mantissas.astype(f32) * scales).astype(bf16)
        noisy_in = (input_weight.astype(f32) + input_noise.astype(f32)).astype(bf16)

        activated, noisy_out, theirs = pl.pallas_call(
            functools.partial(start_kernel, quota),
            out_shape=(shape(2, 2 * group, width), shape(width, model), shape(2 * group, model)),
            in_specs=[pl.BlockSpec(memory_space=pltpu.SMEM)] + [whole] * 4,
            out_specs=(whole,) * 3,
            compiler_params=params,
            cost_estimate=pl.CostEstimate(
                flops=tokens * width * model, bytes_accessed=3 * 2**20, transcendentals=2 * tokens * width
            ),
        )(core[None], preactivation, adc_mask, output_weight, output_noise)

        both = dot(pick(activated, core), noisy_out) + from_core(theirs).astype(f32)
        both = both.astype(bf16).reshape(2 * zs, quota, model)
        parts = exchange(both, "row", same_core)

        all_out = of_four(noisy_out).reshape(4 * width, model)
        all_in = of_four(noisy_in)
        place = lax.axis_index("col")
        own = pick(preactivation.reshape(2, cols, 2 * share, width).swapaxes(0, 1), place)
        own_mask = pick(adc_mask.reshape(2, cols, 2 * share, -1).swapaxes(0, 1), place)
        own_mask = own_mask.reshape(4 * share, -1)
        own = own.reshape(4 * share, width).astype(f32)
        slope = jax.vjp(lambda v: activation(v, own_mask), own)[1](jnp.ones_like(own))[0]
        slope = slope.reshape(2, share // quota, 2, quota, width).swapaxes(1, 2)
        slope = slope.reshape(2, 2, share, width)
        slope = jnp.stack([pick(slope, y), from_y(pick(slope, 1 - y))], axis=1)
        slope = jnp.concatenate([pick(slope, core), from_core(pick(slope, 1 - core))])
        slope = slope.swapaxes(0, 1).reshape(share, 4 * width)

        sent = pl.pallas_call(
            residual_kernel,
            out_shape=shape(zs, 2 * quota, model),
            in_specs=[whole] * 3 + [anywhere] * 2,
            out_specs=whole,
            compiler_params=params,
            cost_estimate=pl.CostEstimate(flops=2**18, bytes_accessed=2**20, transcendentals=0),
        )(parts, teacher, features, all_out, slope)
        got = exchange(sent, "row", along_z)
        piece = got[:, :quota].reshape(group, model)
        fresh = dot_t(piece, all_out).astype(bf16).reshape(cols, share, 4 * width)
        own_grad = (add_up(exchange(fresh, "col")) * slope).astype(bf16)
        hidden_grad = spread(own_grad, cols, "col").reshape(group, 4 * width)

        own_rows = pl.pallas_call(
            rows_kernel,
            out_shape=shape(group, 2 * model),
            in_specs=[whole],
            out_specs=whole,
            compiler_params=params,
            cost_estimate=pl.CostEstimate(flops=0, bytes_accessed=2**20, transcendentals=0),
        )(got)
        partial, for_y, for_core, for_both = pl.pallas_call(
            input_kernel,
            out_shape=(shape(group, model),) + (shape(group, width),) * 3,
            in_specs=[whole] * 5,
            out_specs=(whole,) * 4,
            compiler_params=params,
            cost_estimate=pl.CostEstimate(
                flops=8 * group * width * model, bytes_accessed=3 * 2**20, transcendentals=0
            ),
        )(hidden_grad, *[all_in[i] for i in range(4)])
        partial = partial.reshape(zs, quota, model)
        input_grad = add_up(exchange(partial, "row", along_z)).astype(bf16)

        near_rows = pl.pallas_call(
            pair_kernel,
            out_shape=shape(2, group, 2 * model),
            in_specs=[whole] * 2 + [anywhere],
            out_specs=whole,
            compiler_params=params,
            cost_estimate=pl.CostEstimate(flops=0, bytes_accessed=3 * 2**19, transcendentals=0),
        )(own_rows, from_y(own_rows), partial)
        first_grad, second_grad = pl.pallas_call(
            functools.partial(grads_kernel, inverse_root),
            out_shape=(shape(model, width), shape(width, model)),
            in_specs=[scalar] + [whole] * 7,
            out_specs=(whole,) * 2,
            compiler_params=params,
            cost_estimate=pl.CostEstimate(
                flops=4 * tokens * width * model, bytes_accessed=2**21, transcendentals=0
            ),
        )(
            jnp.stack([core, y]),
            activated.reshape(2, 2, group, width),
            hidden_grad,
            near_rows,
            from_core(near_rows),
            from_y(for_y),
            from_core(for_core),
            from_both(for_both),
        )
        return (input_grad, first_grad, second_grad)

    return local


def solution(mesh):
    placed = (
        P("row", "col"),
        P("row", "col"),
        P("col", "row"),
        P("col", "row"),
        P("row", "col"),
        P("row", "col"),
        P(None, "row"),
        P(None, "row"),
        P("row", "col"),
    )
    return jax.shard_map(
        program(mesh.shape["row"], mesh.shape["col"]),
        mesh=mesh,
        in_specs=placed,
        out_specs=(P("row", "col"), P("col", "row"), P("row", "col")),
        check_vma=False,
    )
```

```python
import functools

import jax
import jax.numpy as jnp
from jax import lax
from jax.experimental import pallas as pl
from jax.experimental.pallas import tpu as pltpu
from jax.sharding import PartitionSpec as P

adc_range = 1.5
bf16 = jnp.bfloat16
f32 = jnp.float32


def activation(hidden, mask):
    width = hidden.shape[1] // mask.shape[1]
    gelu = jax.nn.gelu(hidden, approximate=True)
    tiles = jnp.repeat(mask, width, axis=1)
    return jnp.where(tiles > 0, adc_range * jnp.tanh(gelu / adc_range), gelu)


def dot(a, b):
    return jnp.dot(a, b, preferred_element_type=f32)


def dot_t(a, b):
    return lax.dot_general(a, b, (((1,), (1,)), ((), ())), preferred_element_type=f32)


def t_dot(a, b):
    return lax.dot_general(a, b, (((0,), (0,)), ((), ())), preferred_element_type=f32)


def pick(a, i):
    return lax.dynamic_index_in_dim(a, i, 0, False)


whole = pl.BlockSpec(memory_space=pltpu.VMEM)
scalar = pl.BlockSpec(memory_space=pltpu.SMEM)
anywhere = pl.BlockSpec(memory_space=pl.ANY)
params = pltpu.CompilerParams(vmem_limit_bytes=40 * 2**20)


def shape(*dims):
    return jax.ShapeDtypeStruct(dims, bf16)


def start_kernel(quota, core_ref, pre_ref, mask_ref, w_ref, n_ref, act_ref, out_ref, theirs_ref):
    out_ref[...] = (w_ref[...].astype(f32) + n_ref[...].astype(f32)).astype(bf16)
    tokens, width = pre_ref.shape
    tiles = mask_ref.shape[1]
    tile = width // tiles
    step = min(128, tokens)
    for first in range(0, tokens, step):
        for j in range(tiles):
            columns = slice(j * tile, (j + 1) * tile)
            hidden = pre_ref[first : first + step, columns].astype(f32)
            gelu = jax.nn.gelu(hidden, approximate=True)
            value = jnp.where(
                mask_ref[first : first + step, j : j + 1] > 0,
                adc_range * jnp.tanh(gelu / adc_range),
                gelu,
            )
            value = value.reshape(step // (2 * quota), 2, quota, tile)
            for c in range(2):
                part = value[:, c].reshape(step // 2, tile).astype(bf16)
                act_ref[c, first // 2 : (first + step) // 2, columns] = part
    theirs = dot(act_ref[1 - core_ref[0]], out_ref[...])
    theirs_ref[...] = theirs.astype(bf16)


def residual_kernel(parts_ref, teacher_ref, features_ref, *refs):
    out_ref = refs[-1]
    total = parts_ref[0].astype(f32)
    for i in range(1, parts_ref.shape[0]):
        total += parts_ref[i].astype(f32)
    residual = (total - teacher_ref[...].astype(f32)).astype(bf16)
    block = jnp.concatenate([residual.astype(f32), features_ref[...].astype(f32)]).astype(bf16)
    for i in range(out_ref.shape[0]):
        out_ref[i] = block


def rows_kernel(got_ref, rows_ref):
    count, twice, model = got_ref.shape
    got = got_ref[...].astype(f32)
    for i in range(2):
        half = got[:, i * twice // 2 : (i + 1) * twice // 2].reshape(count * twice // 2, model)
        rows_ref[:, i * model : (i + 1) * model] = half.astype(bf16)


def input_kernel(grad_ref, a_ref, b_ref, c_ref, d_ref, partial_ref, *refs):
    width = a_ref.shape[1]
    block = [grad_ref[:, i * width : (i + 1) * width] for i in range(4)]
    total = dot_t(block[0], a_ref[...])
    for one, ref in zip(block[1:], (b_ref, c_ref, d_ref)):
        total += dot_t(one, ref[...])
    partial_ref[...] = total.astype(bf16)
    for one, ref in zip(block[1:], refs):
        ref[...] = one


def sum_kernel(parts_ref, after_ref, out_ref):
    total = parts_ref[0].astype(f32)
    for i in range(1, parts_ref.shape[0]):
        total += parts_ref[i].astype(f32)
    out_ref[...] = total.astype(bf16)


def later_kernel(a_ref, after_ref, again_ref):
    again_ref[...] = a_ref[...]


def grads_kernel(scale, at_ref, act_ref, grad_ref, *refs):
    *rows, y_ref, core_ref, both_ref, first_ref, second_ref = refs
    width, model = second_ref.shape
    c, y = at_ref[0], at_ref[1]
    act = [act_ref[c, y], act_ref[c, 1 - y], act_ref[1 - c, y], act_ref[1 - c, 1 - y]]
    residual = [ref[:, :model] for ref in rows]
    features = [ref[:, model:] for ref in rows]
    grad = [grad_ref[:, :width]] + [ref[...] for ref in (y_ref, core_ref, both_ref)]
    second = t_dot(jnp.concatenate(act), jnp.concatenate(residual))
    second_ref[...] = (second * scale).astype(bf16)
    first = t_dot(jnp.concatenate(features), jnp.concatenate(grad))
    first_ref[...] = (first * scale).astype(bf16)


def program(rows, cols):
    zs = rows // 4
    same_core = [[chip * 2 + core for chip in range(2 * zs)] for core in range(2)]
    along_z = [[(y * zs + z) * 2 + core for z in range(zs)] for y in range(2) for core in range(2)]
    swap_core = [(i, i ^ 1) for i in range(rows)]
    swap_both = [(i, (i ^ 1) + (rows // 2 if i < rows // 2 else -(rows // 2))) for i in range(rows)]
    swap_y = [(i, (i + rows // 2) % rows) for i in range(rows)]

    def from_core(a):
        return lax.ppermute(a, "row", swap_core)

    def from_y(a):
        return lax.ppermute(a, "row", swap_y)

    def from_both(a):
        return lax.ppermute(a, "row", swap_both)

    def exchange(a, axis, groups=None):
        return lax.all_to_all(a, axis, 0, 0, axis_index_groups=groups, tiled=True)

    def spread(own, count, axis, groups=None):
        return exchange(jnp.broadcast_to(own, (count,) + own.shape), axis, groups)

    def add_up(parts):
        return jnp.sum(parts.astype(f32), axis=0)

    def of_four(own):
        pair = jnp.stack([own, from_y(own)])
        return jnp.concatenate([pair, from_core(pair)])

    def local(
        mantissas,
        block_exponents,
        input_weight,
        input_noise,
        output_weight,
        output_noise,
        preactivation,
        adc_mask,
        teacher,
    ):
        me = lax.axis_index("row")
        core, y = me % 2, me // (rows // 2)
        tokens, width = preactivation.shape
        model = mantissas.shape[1]
        quota = tokens // rows
        group = tokens // 4
        share = group // cols
        inverse_root = tokens ** (-0.5)

        block_width = model // block_exponents.shape[1]
        scales = jnp.repeat(jnp.exp2(block_exponents.astype(f32)), block_width, axis=1)
        features = (mantissas.astype(f32) * scales).astype(bf16)
        noisy_in = (input_weight.astype(f32) + input_noise.astype(f32)).astype(bf16)

        activated, noisy_out, theirs = pl.pallas_call(
            functools.partial(start_kernel, quota),
            out_shape=(shape(2, 2 * group, width), shape(width, model), shape(2 * group, model)),
            in_specs=[pl.BlockSpec(memory_space=pltpu.SMEM)] + [whole] * 4,
            out_specs=(whole,) * 3,
            compiler_params=params,
            cost_estimate=pl.CostEstimate(
                flops=tokens * width * model, bytes_accessed=3 * 2**20, transcendentals=2 * tokens * width
            ),
        )(core[None], preactivation, adc_mask, output_weight, output_noise)

        both = dot(pick(activated, core), noisy_out) + from_core(theirs).astype(f32)
        both = both.astype(bf16).reshape(2 * zs, quota, model)
        parts = exchange(both, "row", same_core)

        all_out = of_four(noisy_out).reshape(4 * width, model)
        all_in = of_four(noisy_in)
        place = lax.axis_index("col")
        own = pick(preactivation.reshape(2, cols, 2 * share, width).swapaxes(0, 1), place)
        own_mask = pick(adc_mask.reshape(2, cols, 2 * share, -1).swapaxes(0, 1), place)
        own_mask = own_mask.reshape(4 * share, -1)
        own = own.reshape(4 * share, width).astype(f32)
        slope = jax.vjp(lambda v: activation(v, own_mask), own)[1](jnp.ones_like(own))[0]
        slope = slope.reshape(2, share // quota, 2, quota, width).swapaxes(1, 2)
        slope = slope.reshape(2, 2, share, width)
        slope = jnp.stack([pick(slope, y), from_y(pick(slope, 1 - y))], axis=1)
        slope = jnp.concatenate([pick(slope, core), from_core(pick(slope, 1 - core))])
        slope = slope.swapaxes(0, 1).reshape(share, 4 * width)

        sent = pl.pallas_call(
            residual_kernel,
            out_shape=shape(zs, 2 * quota, model),
            in_specs=[whole] * 3 + [anywhere] * 2,
            out_specs=whole,
            compiler_params=params,
            cost_estimate=pl.CostEstimate(flops=2**18, bytes_accessed=2**20, transcendentals=0),
        )(parts, teacher, features, all_out, slope)
        got = exchange(sent, "row", along_z)
        piece = got[:, :quota].reshape(group, model)
        fresh = dot_t(piece, all_out).astype(bf16).reshape(cols, share, 4 * width)
        own_grad = (add_up(exchange(fresh, "col")) * slope).astype(bf16)
        hidden_grad = spread(own_grad, cols, "col").reshape(group, 4 * width)

        own_rows = pl.pallas_call(
            rows_kernel,
            out_shape=shape(group, 2 * model),
            in_specs=[whole],
            out_specs=whole,
            compiler_params=params,
            cost_estimate=pl.CostEstimate(flops=0, bytes_accessed=2**20, transcendentals=0),
        )(got)
        partial, for_y, for_core, for_both = pl.pallas_call(
            input_kernel,
            out_shape=(shape(group, model),) + (shape(group, width),) * 3,
            in_specs=[whole] * 5,
            out_specs=(whole,) * 4,
            compiler_params=params,
            cost_estimate=pl.CostEstimate(
                flops=8 * group * width * model, bytes_accessed=3 * 2**20, transcendentals=0
            ),
        )(hidden_grad, *[all_in[i] for i in range(4)])
        partial = partial.reshape(zs, quota, model)
        last = exchange(partial, "row", along_z)

        y_rows = from_y(own_rows)
        later_rows = pl.pallas_call(
            later_kernel,
            out_shape=shape(group, 2 * model),
            in_specs=[whole, anywhere],
            out_specs=whole,
            compiler_params=params,
            cost_estimate=pl.CostEstimate(flops=0, bytes_accessed=2**18, transcendentals=0),
        )(y_rows, partial)
        first_grad, second_grad = pl.pallas_call(
            functools.partial(grads_kernel, inverse_root),
            out_shape=(shape(model, width), shape(width, model)),
            in_specs=[scalar] + [whole] * 9,
            out_specs=(whole,) * 2,
            compiler_params=params,
            cost_estimate=pl.CostEstimate(
                flops=4 * tokens * width * model, bytes_accessed=2**18, transcendentals=0
            ),
        )(
            jnp.stack([core, y]),
            activated.reshape(2, 2, group, width),
            hidden_grad,
            own_rows,
            y_rows,
            from_core(own_rows),
            from_core(later_rows),
            from_y(for_y),
            from_core(for_core),
            from_both(for_both),
        )
        input_grad = pl.pallas_call(
            sum_kernel,
            out_shape=shape(quota, model),
            in_specs=[whole, anywhere],
            out_specs=whole,
            compiler_params=params,
            cost_estimate=pl.CostEstimate(flops=2**17, bytes_accessed=2**18, transcendentals=0),
        )(last, first_grad)
        return (input_grad, first_grad, second_grad)

    return local


def solution(mesh):
    placed = (
        P("row", "col"),
        P("row", "col"),
        P("col", "row"),
        P("col", "row"),
        P("row", "col"),
        P("row", "col"),
        P(None, "row"),
        P(None, "row"),
        P("row", "col"),
    )
    return jax.shard_map(
        program(mesh.shape["row"], mesh.shape["col"]),
        mesh=mesh,
        in_specs=placed,
        out_specs=(P("row", "col"), P("col", "row"), P("row", "col")),
        check_vma=False,
    )
```

```python
import functools

import jax
import jax.numpy as jnp
from jax import lax
from jax.experimental import pallas as pl
from jax.experimental.pallas import tpu as pltpu
from jax.sharding import PartitionSpec as P

adc_range = 1.5
bf16 = jnp.bfloat16
f32 = jnp.float32


def activation(hidden, mask):
    width = hidden.shape[1] // mask.shape[1]
    gelu = jax.nn.gelu(hidden, approximate=True)
    tiles = jnp.repeat(mask, width, axis=1)
    return jnp.where(tiles > 0, adc_range * jnp.tanh(gelu / adc_range), gelu)


def dot(a, b):
    return jnp.dot(a, b, preferred_element_type=f32)


def dot_t(a, b):
    return lax.dot_general(a, b, (((1,), (1,)), ((), ())), preferred_element_type=f32)


def t_dot(a, b):
    return lax.dot_general(a, b, (((0,), (0,)), ((), ())), preferred_element_type=f32)


def pick(a, i):
    return lax.dynamic_index_in_dim(a, i, 0, False)


whole = pl.BlockSpec(memory_space=pltpu.VMEM)
scalar = pl.BlockSpec(memory_space=pltpu.SMEM)
anywhere = pl.BlockSpec(memory_space=pl.ANY)
params = pltpu.CompilerParams(vmem_limit_bytes=40 * 2**20)


def shape(*dims):
    return jax.ShapeDtypeStruct(dims, bf16)


def start_kernel(quota, core_ref, pre_ref, mask_ref, w_ref, n_ref, act_ref, out_ref, theirs_ref):
    out_ref[...] = (w_ref[...].astype(f32) + n_ref[...].astype(f32)).astype(bf16)
    tokens, width = pre_ref.shape
    tiles = mask_ref.shape[1]
    tile = width // tiles
    step = min(128, tokens)
    for first in range(0, tokens, step):
        for j in range(tiles):
            columns = slice(j * tile, (j + 1) * tile)
            hidden = pre_ref[first : first + step, columns].astype(f32)
            gelu = jax.nn.gelu(hidden, approximate=True)
            value = jnp.where(
                mask_ref[first : first + step, j : j + 1] > 0,
                adc_range * jnp.tanh(gelu / adc_range),
                gelu,
            )
            value = value.reshape(step // (2 * quota), 2, quota, tile)
            for c in range(2):
                part = value[:, c].reshape(step // 2, tile).astype(bf16)
                act_ref[c, first // 2 : (first + step) // 2, columns] = part
    theirs = dot(act_ref[1 - core_ref[0]], out_ref[...])
    theirs_ref[...] = theirs.astype(bf16)


def residual_kernel(parts_ref, teacher_ref, features_ref, *refs):
    out_ref = refs[-1]
    total = parts_ref[0].astype(f32)
    for i in range(1, parts_ref.shape[0]):
        total += parts_ref[i].astype(f32)
    residual = (total - teacher_ref[...].astype(f32)).astype(bf16)
    block = jnp.concatenate([residual.astype(f32), features_ref[...].astype(f32)]).astype(bf16)
    for i in range(out_ref.shape[0]):
        out_ref[i] = block


def rows_kernel(got_ref, rows_ref):
    count, twice, model = got_ref.shape
    got = got_ref[...].astype(f32)
    for i in range(2):
        half = got[:, i * twice // 2 : (i + 1) * twice // 2].reshape(count * twice // 2, model)
        rows_ref[:, i * model : (i + 1) * model] = half.astype(bf16)


def input_kernel(grad_ref, a_ref, b_ref, c_ref, d_ref, partial_ref, *refs):
    width = a_ref.shape[1]
    block = [grad_ref[:, i * width : (i + 1) * width] for i in range(4)]
    total = dot_t(block[0], a_ref[...])
    for one, ref in zip(block[1:], (b_ref, c_ref, d_ref)):
        total += dot_t(one, ref[...])
    partial_ref[...] = total.astype(bf16)
    for one, ref in zip(block[1:], refs):
        ref[...] = one


def sum_kernel(parts_ref, after_ref, out_ref):
    total = parts_ref[0].astype(f32)
    for i in range(1, parts_ref.shape[0]):
        total += parts_ref[i].astype(f32)
    out_ref[...] = total.astype(bf16)


def later_kernel(a_ref, after_ref, again_ref):
    again_ref[...] = a_ref[...]


def grads_kernel(scale, at_ref, act_ref, grad_ref, *refs):
    *rows, y_ref, core_ref, both_ref, first_ref, second_ref, done_ref = refs
    width, model = second_ref.shape
    c, y = at_ref[0], at_ref[1]
    act = [act_ref[c, y], act_ref[c, 1 - y], act_ref[1 - c, y], act_ref[1 - c, 1 - y]]
    residual = [ref[:, :model] for ref in rows]
    features = [ref[:, model:] for ref in rows]
    grad = [grad_ref[:, :width]] + [ref[...] for ref in (y_ref, core_ref, both_ref)]
    second = t_dot(jnp.concatenate(act), jnp.concatenate(residual))
    second_ref[...] = (second * scale).astype(bf16)
    first = t_dot(jnp.concatenate(features), jnp.concatenate(grad))
    first_ref[...] = (first * scale).astype(bf16)
    done_ref[...] = jnp.zeros_like(done_ref)


def program(rows, cols):
    zs = rows // 4
    same_core = [[chip * 2 + core for chip in range(2 * zs)] for core in range(2)]
    along_z = [[(y * zs + z) * 2 + core for z in range(zs)] for y in range(2) for core in range(2)]
    swap_core = [(i, i ^ 1) for i in range(rows)]
    swap_both = [(i, (i ^ 1) + (rows // 2 if i < rows // 2 else -(rows // 2))) for i in range(rows)]
    swap_y = [(i, (i + rows // 2) % rows) for i in range(rows)]

    def from_core(a):
        return lax.ppermute(a, "row", swap_core)

    def from_y(a):
        return lax.ppermute(a, "row", swap_y)

    def from_both(a):
        return lax.ppermute(a, "row", swap_both)

    def exchange(a, axis, groups=None):
        return lax.all_to_all(a, axis, 0, 0, axis_index_groups=groups, tiled=True)

    def spread(own, count, axis, groups=None):
        return exchange(jnp.broadcast_to(own, (count,) + own.shape), axis, groups)

    def add_up(parts):
        return jnp.sum(parts.astype(f32), axis=0)

    def of_four(own):
        pair = jnp.stack([own, from_y(own)])
        return jnp.concatenate([pair, from_core(pair)])

    def local(
        mantissas,
        block_exponents,
        input_weight,
        input_noise,
        output_weight,
        output_noise,
        preactivation,
        adc_mask,
        teacher,
    ):
        me = lax.axis_index("row")
        core, y = me % 2, me // (rows // 2)
        tokens, width = preactivation.shape
        model = mantissas.shape[1]
        quota = tokens // rows
        group = tokens // 4
        share = group // cols
        inverse_root = tokens ** (-0.5)

        block_width = model // block_exponents.shape[1]
        scales = jnp.repeat(jnp.exp2(block_exponents.astype(f32)), block_width, axis=1)
        features = (mantissas.astype(f32) * scales).astype(bf16)
        noisy_in = (input_weight.astype(f32) + input_noise.astype(f32)).astype(bf16)

        activated, noisy_out, theirs = pl.pallas_call(
            functools.partial(start_kernel, quota),
            out_shape=(shape(2, 2 * group, width), shape(width, model), shape(2 * group, model)),
            in_specs=[pl.BlockSpec(memory_space=pltpu.SMEM)] + [whole] * 4,
            out_specs=(whole,) * 3,
            compiler_params=params,
            cost_estimate=pl.CostEstimate(
                flops=tokens * width * model, bytes_accessed=3 * 2**20, transcendentals=2 * tokens * width
            ),
        )(core[None], preactivation, adc_mask, output_weight, output_noise)

        both = dot(pick(activated, core), noisy_out) + from_core(theirs).astype(f32)
        both = both.astype(bf16).reshape(2 * zs, quota, model)
        parts = exchange(both, "row", same_core)

        all_out = of_four(noisy_out).reshape(4 * width, model)
        all_in = of_four(noisy_in)
        place = lax.axis_index("col")
        own = pick(preactivation.reshape(2, cols, 2 * share, width).swapaxes(0, 1), place)
        own_mask = pick(adc_mask.reshape(2, cols, 2 * share, -1).swapaxes(0, 1), place)
        own_mask = own_mask.reshape(4 * share, -1)
        own = own.reshape(4 * share, width).astype(f32)
        slope = jax.vjp(lambda v: activation(v, own_mask), own)[1](jnp.ones_like(own))[0]
        slope = slope.reshape(2, share // quota, 2, quota, width).swapaxes(1, 2)
        slope = slope.reshape(2, 2, share, width)
        slope = jnp.stack([pick(slope, y), from_y(pick(slope, 1 - y))], axis=1)
        slope = jnp.concatenate([pick(slope, core), from_core(pick(slope, 1 - core))])
        slope = slope.swapaxes(0, 1).reshape(share, 4 * width)

        sent = pl.pallas_call(
            residual_kernel,
            out_shape=shape(zs, 2 * quota, model),
            in_specs=[whole] * 3 + [anywhere] * 2,
            out_specs=whole,
            compiler_params=params,
            cost_estimate=pl.CostEstimate(flops=2**18, bytes_accessed=2**20, transcendentals=0),
        )(parts, teacher, features, all_out, slope)
        got = exchange(sent, "row", along_z)
        piece = got[:, :quota].reshape(group, model)
        fresh = dot_t(piece, all_out).astype(bf16).reshape(cols, share, 4 * width)
        own_grad = (add_up(exchange(fresh, "col")) * slope).astype(bf16)
        hidden_grad = spread(own_grad, cols, "col").reshape(group, 4 * width)

        own_rows = pl.pallas_call(
            rows_kernel,
            out_shape=shape(group, 2 * model),
            in_specs=[whole],
            out_specs=whole,
            compiler_params=params,
            cost_estimate=pl.CostEstimate(flops=0, bytes_accessed=2**20, transcendentals=0),
        )(got)
        partial, for_y, for_core, for_both = pl.pallas_call(
            input_kernel,
            out_shape=(shape(group, model),) + (shape(group, width),) * 3,
            in_specs=[whole] * 5,
            out_specs=(whole,) * 4,
            compiler_params=params,
            cost_estimate=pl.CostEstimate(
                flops=8 * group * width * model, bytes_accessed=3 * 2**20, transcendentals=0
            ),
        )(hidden_grad, *[all_in[i] for i in range(4)])
        partial = partial.reshape(zs, quota, model)
        last = exchange(partial, "row", along_z)

        y_rows = from_y(own_rows)
        later_rows = pl.pallas_call(
            later_kernel,
            out_shape=shape(group, 2 * model),
            in_specs=[whole, anywhere],
            out_specs=whole,
            compiler_params=params,
            cost_estimate=pl.CostEstimate(flops=0, bytes_accessed=2**18, transcendentals=0),
        )(y_rows, partial)
        first_grad, second_grad, done = pl.pallas_call(
            functools.partial(grads_kernel, inverse_root),
            out_shape=(shape(model, width), shape(width, model), shape(16, 128)),
            in_specs=[scalar] + [whole] * 9,
            out_specs=(whole,) * 3,
            compiler_params=params,
            cost_estimate=pl.CostEstimate(
                flops=4 * tokens * width * model, bytes_accessed=2**18, transcendentals=0
            ),
        )(
            jnp.stack([core, y]),
            activated.reshape(2, 2, group, width),
            hidden_grad,
            own_rows,
            y_rows,
            from_core(own_rows),
            from_core(later_rows),
            from_y(for_y),
            from_core(for_core),
            from_both(for_both),
        )
        input_grad = pl.pallas_call(
            sum_kernel,
            out_shape=shape(quota, model),
            in_specs=[whole, anywhere],
            out_specs=whole,
            compiler_params=params,
            cost_estimate=pl.CostEstimate(flops=2**17, bytes_accessed=2**18, transcendentals=0),
        )(last, done)
        return (input_grad, first_grad, second_grad)

    return local


def solution(mesh):
    placed = (
        P("row", "col"),
        P("row", "col"),
        P("col", "row"),
        P("col", "row"),
        P("row", "col"),
        P("row", "col"),
        P(None, "row"),
        P(None, "row"),
        P("row", "col"),
    )
    return jax.shard_map(
        program(mesh.shape["row"], mesh.shape["col"]),
        mesh=mesh,
        in_specs=placed,
        out_specs=(P("row", "col"), P("col", "row"), P("row", "col")),
        check_vma=False,
    )
```

```python
import functools

import jax
import jax.numpy as jnp
from jax import lax
from jax.experimental import pallas as pl
from jax.experimental.pallas import tpu as pltpu
from jax.sharding import PartitionSpec as P

adc_range = 1.5
bf16 = jnp.bfloat16
f32 = jnp.float32


def activation(hidden, mask):
    width = hidden.shape[1] // mask.shape[1]
    gelu = jax.nn.gelu(hidden, approximate=True)
    tiles = jnp.repeat(mask, width, axis=1)
    return jnp.where(tiles > 0, adc_range * jnp.tanh(gelu / adc_range), gelu)


def dot(a, b):
    return jnp.dot(a, b, preferred_element_type=f32)


def dot_t(a, b):
    return lax.dot_general(a, b, (((1,), (1,)), ((), ())), preferred_element_type=f32)


def t_dot(a, b):
    return lax.dot_general(a, b, (((0,), (0,)), ((), ())), preferred_element_type=f32)


def pick(a, i):
    return lax.dynamic_index_in_dim(a, i, 0, False)


whole = pl.BlockSpec(memory_space=pltpu.VMEM)
scalar = pl.BlockSpec(memory_space=pltpu.SMEM)
anywhere = pl.BlockSpec(memory_space=pl.ANY)
params = pltpu.CompilerParams(vmem_limit_bytes=40 * 2**20)


def shape(*dims):
    return jax.ShapeDtypeStruct(dims, bf16)


def start_kernel(quota, core_ref, pre_ref, mask_ref, w_ref, n_ref, act_ref, out_ref, theirs_ref):
    out_ref[...] = (w_ref[...].astype(f32) + n_ref[...].astype(f32)).astype(bf16)
    tokens, width = pre_ref.shape
    tiles = mask_ref.shape[1]
    tile = width // tiles
    step = min(128, tokens)
    for first in range(0, tokens, step):
        for j in range(tiles):
            columns = slice(j * tile, (j + 1) * tile)
            hidden = pre_ref[first : first + step, columns].astype(f32)
            gelu = jax.nn.gelu(hidden, approximate=True)
            value = jnp.where(
                mask_ref[first : first + step, j : j + 1] > 0,
                adc_range * jnp.tanh(gelu / adc_range),
                gelu,
            )
            value = value.reshape(step // (2 * quota), 2, quota, tile)
            for c in range(2):
                part = value[:, c].reshape(step // 2, tile).astype(bf16)
                act_ref[c, first // 2 : (first + step) // 2, columns] = part
    theirs = dot(act_ref[1 - core_ref[0]], out_ref[...])
    theirs_ref[...] = theirs.astype(bf16)


def residual_kernel(parts_ref, teacher_ref, features_ref, *refs):
    out_ref = refs[-1]
    total = parts_ref[0].astype(f32)
    for i in range(1, parts_ref.shape[0]):
        total += parts_ref[i].astype(f32)
    residual = (total - teacher_ref[...].astype(f32)).astype(bf16)
    block = jnp.concatenate([residual.astype(f32), features_ref[...].astype(f32)]).astype(bf16)
    for i in range(out_ref.shape[0]):
        out_ref[i] = block


def rows_kernel(got_ref, rows_ref):
    count, twice, model = got_ref.shape
    got = got_ref[...].astype(f32)
    for i in range(2):
        half = got[:, i * twice // 2 : (i + 1) * twice // 2].reshape(count * twice // 2, model)
        rows_ref[:, i * model : (i + 1) * model] = half.astype(bf16)


def input_kernel(grad_ref, a_ref, b_ref, c_ref, d_ref, partial_ref, *refs):
    width = a_ref.shape[1]
    block = [grad_ref[:, i * width : (i + 1) * width] for i in range(4)]
    total = dot_t(block[0], a_ref[...])
    for one, ref in zip(block[1:], (b_ref, c_ref, d_ref)):
        total += dot_t(one, ref[...])
    partial_ref[...] = total.astype(bf16)
    for one, ref in zip(block[1:], refs):
        ref[...] = one


def sum_kernel(parts_ref, after_ref, out_ref):
    total = parts_ref[0].astype(f32)
    for i in range(1, parts_ref.shape[0]):
        total += parts_ref[i].astype(f32)
    out_ref[...] = total.astype(bf16)


def later_kernel(a_ref, after_ref, again_ref):
    again_ref[...] = a_ref[...]


def grads_kernel(scale, at_ref, act_ref, grad_ref, *refs):
    *rows, y_ref, core_ref, both_ref, first_ref, second_ref, done_ref = refs
    width, model = second_ref.shape
    c, y = at_ref[0], at_ref[1]
    act = [act_ref[c, y], act_ref[c, 1 - y], act_ref[1 - c, y], act_ref[1 - c, 1 - y]]
    residual = [ref[:, :model] for ref in rows]
    features = [ref[:, model:] for ref in rows]
    grad = [grad_ref[:, :width]] + [ref[...] for ref in (y_ref, core_ref, both_ref)]
    second = t_dot(jnp.concatenate(act), jnp.concatenate(residual))
    second_ref[...] = (second * scale).astype(bf16)
    first = t_dot(jnp.concatenate(features), jnp.concatenate(grad))
    first_ref[...] = (first * scale).astype(bf16)
    done_ref[...] = jnp.zeros_like(done_ref)


def program(rows, cols):
    zs = rows // 4
    same_core = [[chip * 2 + core for chip in range(2 * zs)] for core in range(2)]
    along_z = [[(y * zs + z) * 2 + core for z in range(zs)] for y in range(2) for core in range(2)]
    swap_core = [(i, i ^ 1) for i in range(rows)]
    swap_both = [(i, (i ^ 1) + (rows // 2 if i < rows // 2 else -(rows // 2))) for i in range(rows)]
    swap_y = [(i, (i + rows // 2) % rows) for i in range(rows)]

    def from_core(a):
        return lax.ppermute(a, "row", swap_core)

    def from_y(a):
        return lax.ppermute(a, "row", swap_y)

    def from_both(a):
        return lax.ppermute(a, "row", swap_both)

    def exchange(a, axis, groups=None):
        return lax.all_to_all(a, axis, 0, 0, axis_index_groups=groups, tiled=True)

    def spread(own, count, axis, groups=None):
        return exchange(jnp.broadcast_to(own, (count,) + own.shape), axis, groups)

    def add_up(parts):
        return jnp.sum(parts.astype(f32), axis=0)

    def of_four(own):
        pair = jnp.stack([own, from_y(own)])
        return jnp.concatenate([pair, from_core(pair)])

    def local(
        mantissas,
        block_exponents,
        input_weight,
        input_noise,
        output_weight,
        output_noise,
        preactivation,
        adc_mask,
        teacher,
    ):
        me = lax.axis_index("row")
        core, y = me % 2, me // (rows // 2)
        tokens, width = preactivation.shape
        model = mantissas.shape[1]
        quota = tokens // rows
        group = tokens // 4
        share = group // cols
        inverse_root = tokens ** (-0.5)

        block_width = model // block_exponents.shape[1]
        scales = jnp.repeat(jnp.exp2(block_exponents.astype(f32)), block_width, axis=1)
        features = (mantissas.astype(f32) * scales).astype(bf16)
        noisy_in = (input_weight.astype(f32) + input_noise.astype(f32)).astype(bf16)

        activated, noisy_out, theirs = pl.pallas_call(
            functools.partial(start_kernel, quota),
            out_shape=(shape(2, 2 * group, width), shape(width, model), shape(2 * group, model)),
            in_specs=[pl.BlockSpec(memory_space=pltpu.SMEM)] + [whole] * 4,
            out_specs=(whole,) * 3,
            compiler_params=params,
            cost_estimate=pl.CostEstimate(
                flops=tokens * width * model, bytes_accessed=3 * 2**20, transcendentals=2 * tokens * width
            ),
        )(core[None], preactivation, adc_mask, output_weight, output_noise)

        both = dot(pick(activated, core), noisy_out) + from_core(theirs).astype(f32)
        both = both.astype(bf16).reshape(2 * zs, quota, model)
        parts = exchange(both, "row", same_core)

        all_out = of_four(noisy_out).reshape(4 * width, model)
        in_y = from_y(noisy_in)
        place = lax.axis_index("col")
        own = pick(preactivation.reshape(2, cols, 2 * share, width).swapaxes(0, 1), place)
        own_mask = pick(adc_mask.reshape(2, cols, 2 * share, -1).swapaxes(0, 1), place)
        own_mask = own_mask.reshape(4 * share, -1)
        own = own.reshape(4 * share, width).astype(f32)
        slope = jax.vjp(lambda v: activation(v, own_mask), own)[1](jnp.ones_like(own))[0]
        slope = slope.reshape(2, share // quota, 2, quota, width).swapaxes(1, 2)
        slope = slope.reshape(2, 2, share, width)
        slope = jnp.stack([pick(slope, y), from_y(pick(slope, 1 - y))], axis=1)
        slope = jnp.concatenate([pick(slope, core), from_core(pick(slope, 1 - core))])
        slope = slope.swapaxes(0, 1).reshape(share, 4 * width)

        sent = pl.pallas_call(
            residual_kernel,
            out_shape=shape(zs, 2 * quota, model),
            in_specs=[whole] * 3 + [anywhere] * 2,
            out_specs=whole,
            compiler_params=params,
            cost_estimate=pl.CostEstimate(flops=2**18, bytes_accessed=2**20, transcendentals=0),
        )(parts, teacher, features, all_out, slope)
        got = exchange(sent, "row", along_z)
        piece = got[:, :quota].reshape(group, model)
        fresh = dot_t(piece, all_out).astype(bf16).reshape(cols, share, 4 * width)
        own_grad = (add_up(exchange(fresh, "col")) * slope).astype(bf16)
        hidden_grad = spread(own_grad, cols, "col").reshape(group, 4 * width)

        later_in = pl.pallas_call(
            later_kernel,
            out_shape=shape(model, width),
            in_specs=[whole, anywhere],
            out_specs=whole,
            compiler_params=params,
            cost_estimate=pl.CostEstimate(flops=0, bytes_accessed=2**18, transcendentals=0),
        )(in_y, fresh)
        own_rows = pl.pallas_call(
            rows_kernel,
            out_shape=shape(group, 2 * model),
            in_specs=[whole],
            out_specs=whole,
            compiler_params=params,
            cost_estimate=pl.CostEstimate(flops=0, bytes_accessed=2**20, transcendentals=0),
        )(got)
        partial, for_y, for_core, for_both = pl.pallas_call(
            input_kernel,
            out_shape=(shape(group, model),) + (shape(group, width),) * 3,
            in_specs=[whole] * 5,
            out_specs=(whole,) * 4,
            compiler_params=params,
            cost_estimate=pl.CostEstimate(
                flops=8 * group * width * model, bytes_accessed=3 * 2**20, transcendentals=0
            ),
        )(hidden_grad, noisy_in, in_y, from_core(noisy_in), from_core(later_in))
        partial = partial.reshape(zs, quota, model)
        last = exchange(partial, "row", along_z)

        y_rows = from_y(own_rows)
        later_rows = pl.pallas_call(
            later_kernel,
            out_shape=shape(group, 2 * model),
            in_specs=[whole, anywhere],
            out_specs=whole,
            compiler_params=params,
            cost_estimate=pl.CostEstimate(flops=0, bytes_accessed=2**18, transcendentals=0),
        )(y_rows, partial)
        first_grad, second_grad, done = pl.pallas_call(
            functools.partial(grads_kernel, inverse_root),
            out_shape=(shape(model, width), shape(width, model), shape(16, 128)),
            in_specs=[scalar] + [whole] * 9,
            out_specs=(whole,) * 3,
            compiler_params=params,
            cost_estimate=pl.CostEstimate(
                flops=4 * tokens * width * model, bytes_accessed=2**18, transcendentals=0
            ),
        )(
            jnp.stack([core, y]),
            activated.reshape(2, 2, group, width),
            hidden_grad,
            own_rows,
            y_rows,
            from_core(own_rows),
            from_core(later_rows),
            from_y(for_y),
            from_core(for_core),
            from_both(for_both),
        )
        input_grad = pl.pallas_call(
            sum_kernel,
            out_shape=shape(quota, model),
            in_specs=[whole, anywhere],
            out_specs=whole,
            compiler_params=params,
            cost_estimate=pl.CostEstimate(flops=2**17, bytes_accessed=2**18, transcendentals=0),
        )(last, done)
        return (input_grad, first_grad, second_grad)

    return local


def solution(mesh):
    placed = (
        P("row", "col"),
        P("row", "col"),
        P("col", "row"),
        P("col", "row"),
        P("row", "col"),
        P("row", "col"),
        P(None, "row"),
        P(None, "row"),
        P("row", "col"),
    )
    return jax.shard_map(
        program(mesh.shape["row"], mesh.shape["col"]),
        mesh=mesh,
        in_specs=placed,
        out_specs=(P("row", "col"), P("col", "row"), P("row", "col")),
        check_vma=False,
    )
```
